32 devices in a mesh: groups: 2 (over x), shard: 16 (over z, y, core).
Axes of the slice: x: 2, y: 2, z: 4, core: 2. Of those that a mesh axis runs over, the one named last changes fastest.
Arguments:
- embeddings: float32 [8192, 1024], P(('groups', 'shard')), parts along dimension 0, as said below
- dest_owner: int32 [8192], P(('groups', 'shard')), parts along dimension 0, may hold values from 0 to 15, as said below
- member_cluster: int32 [8192], P(('groups', 'shard')), parts along dimension 0, may hold values from 0 to 31
- order: int32 [8192], P(('groups', 'shard')), parts along dimension 0, may hold values from 0 to 4095, each once
Outputs:
- max_similarity: float32 [8192], P(('groups', 'shard')), parts along dimension 0
- centroids: float32 [1024, 1024], P(('groups', 'shard')), parts along dimension 0
The draws below stay inside these ranges and needn't reach their ends.
There are 2 independent parts, one for each index of `groups`. The reference program is written for one: setup_inputs(seed, part) draws one part's arguments, and reference() takes and returns one part's arrays. A program takes and returns all parts, laid end to end along the dimension named above; each array names one. Nothing has to cross between parts.
Inputs may be any that keep to these rules, and one draw needn't show every extreme that they name: `dest_owner`: the rows of one device name any one owner at most 32 times; one owner, the same for all devices of a part, is named exactly 32 times by every device. `order`: each document has its own rank. `embeddings`: rows have norms of widely different sizes.
All inputs are finite; a program needn't handle non-finite values.
Results may differ from the reference program's by a relative error of at most 0.0017.
Values may be sent and summed in bfloat16 or wider, within the bound.
A program may use at most 64 MiB of HBM per device.

```python
import jax
import jax.numpy as jnp
from jax import lax

D = 1024
ROWS_DEV = 256
CL_DEV = 32
CAP = 32
TOTAL = 4096
CLUSTERS = 512
N_SHARD = 16


def placement_ids(key):
    base = jax.random.fold_in(key, 11)
    busiest_key, device_key = jax.random.split(base)
    busiest = jax.random.randint(busiest_key, (), 0, N_SHARD)
    device_keys = jax.random.split(device_key, N_SHARD)

    def per_device(one_key):
        first_key, second_key = jax.random.split(one_key)
        positions = jax.random.permutation(first_key, (N_SHARD - 1) * CAP)[:ROWS_DEV - CAP]
        others = positions // CAP
        others = others + (others >= busiest).astype(others.dtype)
        owners = jnp.concatenate([jnp.full((CAP,), busiest, others.dtype), others])
        return owners[jax.random.permutation(second_key, ROWS_DEV)]
    owners = jax.vmap(per_device)(device_keys).reshape(-1).astype(jnp.int32)
    locals_drawn = jax.random.randint(jax.random.fold_in(key, 12), (TOTAL,), 0, CL_DEV).astype(jnp.int32)
    return (owners, locals_drawn)


def draw_dest_owner(key, part):
    owners, locals_drawn = placement_ids(key)
    return owners


def draw_member_cluster(key, part):
    owners, locals_drawn = placement_ids(key)
    return locals_drawn


def draw_embeddings(key, part):
    owners, locals_drawn = placement_ids(key)
    cluster = owners * CL_DEV + locals_drawn
    key = jax.random.fold_in(key, 5)
    anchor_key, noise_key, scale_key = jax.random.split(key, 3)
    anchors = jax.random.normal(anchor_key, (CLUSTERS, D), jnp.float32)
    noise = jax.random.normal(noise_key, (TOTAL, D), jnp.float32)
    top = 10.0
    scales = jnp.exp(jax.random.uniform(scale_key, (TOTAL, 1), jnp.float32, 0.0, jnp.log(top)))
    return (scales * (noise + anchors[cluster])).astype(jnp.float32)


def setup_inputs(seed: int = 0, part: int = 0) -> dict:
    key_list = jax.random.split(jax.random.key(seed), 5)
    part_splits = jax.random.split(jax.random.fold_in(key_list[4], part), 5)
    return {
        "embeddings": draw_embeddings(jax.random.fold_in(jax.random.fold_in(key_list[4], part), 71), part),
        "dest_owner": draw_dest_owner(jax.random.fold_in(jax.random.fold_in(key_list[4], part), 71), part),
        "member_cluster": draw_member_cluster(jax.random.fold_in(jax.random.fold_in(key_list[4], part), 71), part),
        "order": jax.random.permutation(part_splits[3], TOTAL).astype(jnp.int32),
    }


EPSILON = 1e-06

def reference(embeddings, dest_owner, member_cluster, order):
    squares = lax.optimization_barrier(jnp.sum(embeddings * embeddings, axis=1, keepdims=True))
    unit = (embeddings * lax.rsqrt(squares + EPSILON)).astype(jnp.bfloat16)
    cluster = (dest_owner * CL_DEV + member_cluster).astype(jnp.int32)
    slots = N_SHARD * CAP

    def owner_work(owner):
        found = jnp.nonzero(dest_owner == owner, size=slots, fill_value=TOTAL)[0].astype(jnp.int32)
        valid = found < TOTAL
        safe = jnp.minimum(found, TOTAL - 1).astype(jnp.int32)
        rows = unit[safe]
        row_cluster = jnp.where(valid, cluster[safe], -1)
        row_order = order[safe]
        scores = jnp.dot(rows, rows.T, preferred_element_type=jnp.float32)
        allowed = (row_cluster[:, None] == row_cluster[None, :]) & (row_cluster[None, :] >= 0)
        allowed = allowed & (row_order[None, :] < row_order[:, None])
        best = lax.optimization_barrier(jnp.max(jnp.where(allowed, scores, jnp.float32(-1.0)), axis=1))
        return (found, best)
    found, best = lax.map(owner_work, jnp.arange(N_SHARD, dtype=jnp.int32))
    max_similarity = jnp.full((TOTAL,), -1.0, jnp.float32)
    max_similarity = max_similarity.at[found.reshape(-1)].set(best.reshape(-1), mode='drop')
    sums = jax.ops.segment_sum(unit.astype(jnp.float32), cluster, num_segments=CLUSTERS)
    centroids = sums * lax.rsqrt(lax.optimization_barrier(jnp.mean(sums * sums, axis=1, keepdims=True)) + EPSILON)
    return (max_similarity, centroids)
```

```python
import functools

import jax
import jax.numpy as jnp
from jax import lax
from jax.experimental import pallas as pl
from jax.experimental.pallas import tpu as pltpu
from jax.sharding import PartitionSpec as P

CL_DEV = 32
EPSILON = 1e-06
ORDER_SPAN = 32768
MESH = pl.DeviceIdType.MESH
F32 = jnp.float32
BF16 = jnp.bfloat16


def flipped(me, k):
    peer = me
    bit = 1
    while bit <= k:
        if k & bit:
            peer = peer + bit * (1 - 2 * ((me // bit) % 2))
        bit *= 2
    return peer


def exchange_kernel(
    n, cap,
    emb_ref, dest_ref, member_ref, order_ref,
    best_ref, cent_ref,
    unit, pack, send, recv, keys_out, keys_in, best_out, best_in,
    row_send, row_recv, key_send, key_recv, best_send, best_recv,
):
    me = lax.axis_index("shard")
    rows = emb_ref.shape[0]
    features = emb_ref.shape[1]
    slots = n * cap
    per_tile = 128 // cap
    tiles = slots // 128

    barrier = pltpu.get_barrier_semaphore()
    for k in range(1, n):
        pl.semaphore_signal(
            barrier, inc=1, device_id={"shard": flipped(me, k)}, device_id_type=MESH
        )

    dest = dest_ref[...]
    owner_table = (lax.broadcasted_iota(jnp.int32, (n, rows), 0) == dest).astype(F32)
    before = (
        lax.broadcasted_iota(jnp.int32, (rows, rows), 0)
        < lax.broadcasted_iota(jnp.int32, (rows, rows), 1)
    ).astype(F32).astype(BF16)
    earlier = jnp.dot(owner_table.astype(BF16), before, preferred_element_type=F32)
    rank = jnp.sum(earlier * owner_table, axis=0, keepdims=True).astype(jnp.int32)
    slot = jnp.bitwise_xor(dest, me) * cap + rank
    pack[...] = (
        lax.broadcasted_iota(jnp.int32, (slots, rows), 0) == slot
    ).astype(F32).astype(BF16)

    part = lax.broadcasted_iota(jnp.int32, (8, rows), 0)
    order = order_ref[...]
    fields = jnp.where(
        part == 0,
        member_ref[...] + 1,
        jnp.where(part == 1, order // 128, jnp.where(part == 2, order % 128, 0)),
    ).astype(F32).astype(BF16)
    packed = lax.dot_general(
        fields, pack[...], (((1,), (1,)), ((), ())), preferred_element_type=F32
    )
    key_row = packed[0:1] * float(ORDER_SPAN) + packed[1:2] * 128.0 + packed[2:3]
    for t in range(tiles):
        keys_out[t] = jnp.broadcast_to(key_row[:, t * 128:(t + 1) * 128], (8, 128))

    x = emb_ref[...]
    squares = jnp.sum(x * x, axis=1, keepdims=True)
    unit[...] = (x * lax.rsqrt(squares + EPSILON)).astype(BF16)

    pl.semaphore_wait(barrier, n - 1)

    def copy(src, dst, sems, k):
        return pltpu.make_async_remote_copy(
            src_ref=src, dst_ref=dst, send_sem=sems[0].at[k], recv_sem=sems[1].at[k],
            device_id={"shard": flipped(me, k)}, device_id_type=MESH,
        )

    row_copies, key_copies, best_copies = {}, {}, {}
    for t in reversed(range(tiles)):
        block = jnp.dot(
            pack[t * 128:(t + 1) * 128, :], unit[...], preferred_element_type=F32
        ).astype(BF16)
        send[t * 128:(t + 1) * 128, :] = block
        for k in reversed(range(t * per_tile, (t + 1) * per_tile)):
            if k == 0:
                recv[0:cap, :] = block[0:cap, :]
                continue
            key_copies[k] = copy(keys_out.at[t], keys_in.at[k], (key_send, key_recv), k)
            row_copies[k] = copy(
                send.at[pl.ds(k * cap, cap)], recv.at[pl.ds(k * cap, cap)],
                (row_send, row_recv), k,
            )
            key_copies[k].start()
            row_copies[k].start()

    lane = lax.broadcasted_iota(jnp.int32, (8, 128), 1) // cap

    def gathered(own, arrived):
        result = []
        for t in range(tiles):
            tile = own[t] if t == 0 else arrived[t * per_tile]
            for j in range(1, per_tile):
                tile = jnp.where(lane == j, arrived[t * per_tile + j], tile)
            result.append(tile)
        return result

    for k in range(1, n):
        key_copies[k].wait_recv()
    key_tiles = gathered(keys_out, keys_in)
    key_lanes = jnp.concatenate([tile[0:1] for tile in key_tiles], axis=1)
    cluster_lanes = jnp.floor(key_lanes * (1.0 / ORDER_SPAN))
    base_lanes = cluster_lanes * float(ORDER_SPAN)
    key_cols = [
        jnp.transpose(jnp.broadcast_to(tile[0:1], (128, 128)))[:, 0:1] for tile in key_tiles
    ]

    for k in range(1, n):
        row_copies[k].wait_recv()

    best = jnp.full((1, slots), -1.0, F32)
    for t in range(tiles):
        scores = lax.dot_general(
            recv[t * 128:(t + 1) * 128, :], recv[...], (((1,), (1,)), ((), ())),
            preferred_element_type=F32,
        )
        column = jnp.broadcast_to(key_cols[t], (128, slots))
        allowed = (column < key_lanes) & (column >= base_lanes)
        best = jnp.maximum(
            best, jnp.max(jnp.where(allowed, scores, -1.0), axis=0, keepdims=True)
        )
    for t in range(tiles):
        best_out[t] = jnp.broadcast_to(best[:, t * 128:(t + 1) * 128], (8, 128))
    for k in range(1, n):
        best_copies[k] = copy(
            best_out.at[k // per_tile], best_in.at[k], (best_send, best_recv), k
        )
        best_copies[k].start()

    clusters = cent_ref.shape[0]
    wanted = lax.broadcasted_iota(jnp.int32, (clusters, slots), 0).astype(F32) + 1.0
    member_table = (wanted == cluster_lanes).astype(F32).astype(BF16)
    sums = jnp.dot(member_table, recv[...], preferred_element_type=F32)
    cent_ref[...] = sums * lax.rsqrt(
        jnp.sum(sums * sums, axis=1, keepdims=True) * (1.0 / features) + EPSILON
    )

    for k in range(1, n):
        best_copies[k].wait_recv()
    returned = jnp.concatenate(gathered(best_out, best_in), axis=1)
    result = jnp.zeros((8, rows), F32)
    pieces = []
    for _ in range(3):
        piece = returned.astype(BF16)
        pieces.append(piece)
        returned = returned - piece.astype(F32)
    for piece in pieces:
        result = result + jnp.dot(piece, pack[...], preferred_element_type=F32)
    best_ref[...] = result[0:1]

    for k in range(1, n):
        key_copies[k].wait_send()
        row_copies[k].wait_send()
        best_copies[k].wait_send()


def fused(embeddings, dest_owner, member_cluster, order, n, cap):
    rows, features = embeddings.shape
    slots = n * cap
    vmem = pl.BlockSpec(memory_space=pltpu.VMEM)
    best, centroids = pl.pallas_call(
        functools.partial(exchange_kernel, n, cap),
        out_shape=(
            jax.ShapeDtypeStruct((1, rows), F32),
            jax.ShapeDtypeStruct((CL_DEV, features), F32),
        ),
        in_specs=[vmem] * 4,
        out_specs=(vmem, vmem),
        scratch_shapes=[
            pltpu.VMEM((rows, features), BF16),
            pltpu.VMEM((slots, rows), BF16),
            pltpu.VMEM((slots, features), BF16),
            pltpu.VMEM((slots, features), BF16),
            pltpu.VMEM((slots // 128, 8, 128), F32),
            pltpu.VMEM((n, 8, 128), F32),
            pltpu.VMEM((slots // 128, 8, 128), F32),
            pltpu.VMEM((n, 8, 128), F32),
        ] + [pltpu.SemaphoreType.DMA((n,))] * 6,
        compiler_params=pltpu.CompilerParams(
            collective_id=0, has_side_effects=True, vmem_limit_bytes=32 * 1024 * 1024
        ),
        cost_estimate=pl.CostEstimate(
            flops=2 * slots * features * (rows + slots + CL_DEV),
            bytes_accessed=4 * rows * features,
            transcendentals=rows,
        ),
    )(
        embeddings,
        dest_owner.reshape(1, rows),
        member_cluster.reshape(1, rows),
        order.reshape(1, rows),
    )
    return best.reshape(rows), centroids


def plain(embeddings, dest_owner, member_cluster, order, owners, capacity):
    rows_here, features = embeddings.shape
    slots = owners * capacity
    squares = jnp.sum(embeddings * embeddings, axis=1, keepdims=True)
    unit_rows = (embeddings * lax.rsqrt(squares + EPSILON)).astype(BF16)
    owner_table = (dest_owner[:, None] == jnp.arange(owners, dtype=jnp.int32)[None, :]).astype(F32)
    positions = jnp.arange(rows_here, dtype=jnp.int32)
    before = (positions[:, None] > positions[None, :]).astype(F32)
    earlier = jnp.dot(before, owner_table, precision=lax.Precision.HIGHEST)
    rank = jnp.sum(earlier * owner_table, axis=1).astype(jnp.int32)
    slot_index = dest_owner * capacity + rank
    send_rows = jnp.zeros((slots, features), BF16).at[slot_index].set(unit_rows)
    code = (member_cluster + 1) * ORDER_SPAN + order
    send_code = jnp.zeros((slots,), jnp.int32).at[slot_index].set(code)
    recv_rows = lax.all_to_all(send_rows, "shard", split_axis=0, concat_axis=0, tiled=True)
    recv_code = lax.all_to_all(send_code, "shard", split_axis=0, concat_axis=0, tiled=True)
    recv_cluster = recv_code // ORDER_SPAN
    scores = lax.dot_general(
        recv_rows, recv_rows, (((1,), (1,)), ((), ())), preferred_element_type=F32
    )
    allowed = (recv_cluster[:, None] == recv_cluster[None, :]) & (
        recv_code[None, :] < recv_code[:, None]
    )
    maxima = jnp.max(jnp.where(allowed, scores, F32(-1.0)), axis=1)
    returned = lax.all_to_all(maxima, "shard", split_axis=0, concat_axis=0, tiled=True)
    max_similarity = returned[slot_index]
    wanted = jnp.arange(CL_DEV, dtype=jnp.int32) + 1
    member_table = (wanted[:, None] == recv_cluster[None, :]).astype(BF16)
    sums = jnp.dot(member_table, recv_rows, preferred_element_type=F32)
    centroids = sums * lax.rsqrt(jnp.mean(sums * sums, axis=1, keepdims=True) + EPSILON)
    return (max_similarity, centroids)


def per_device(embeddings, dest_owner, member_cluster, order):
    owners = lax.axis_size("shard")
    capacity = 2 * embeddings.shape[0] // owners
    blocks_tile = capacity % 16 == 0 and 128 % capacity == 0 and owners & (owners - 1) == 0
    body = fused if blocks_tile else plain
    return body(embeddings, dest_owner, member_cluster, order, owners, capacity)


def solution(mesh):
    in_specs = (
        P(("groups", "shard"), None),
        P(("groups", "shard")),
        P(("groups", "shard")),
        P(("groups", "shard")),
    )
    out_specs = (P(("groups", "shard")), P(("groups", "shard"), None))
    return jax.shard_map(
        per_device, mesh=mesh, in_specs=in_specs, out_specs=out_specs, check_vma=False
    )
```

```python
import functools

import jax
import jax.numpy as jnp
from jax import lax
from jax.experimental import pallas as pl
from jax.experimental.pallas import tpu as pltpu
from jax.sharding import PartitionSpec as P

CL_DEV = 32
EPSILON = 1e-06
ORDER_SPAN = 32768
MESH = pl.DeviceIdType.MESH
F32 = jnp.float32
BF16 = jnp.bfloat16


def flipped(me, n):
    steps = []
    bit = 1
    while bit < n:
        steps.append(bit * (1 - 2 * lax.rem(lax.div(me, bit), 2)))
        bit *= 2
    peers = [me]
    for step in steps:
        peers = peers + [peer + step for peer in peers]
    return peers


def exchange_kernel(
    n, cap,
    emb_hbm, dest_hbm, member_hbm, order_hbm,
    best_ref, cent_ref,
    unit, pack, send, recv, keys_out, keys_in, best_out, best_in,
    row_send, row_recv, key_send, key_recv, best_send, best_recv,
    emb_ref, dest_ref, member_ref, order_ref, load_sem,
):
    me = lax.axis_index("shard")
    peers = flipped(me, n)
    loads = [
        pltpu.make_async_copy(src, dst, load_sem.at[i])
        for i, (src, dst) in enumerate(
            [
                (dest_hbm, dest_ref), (member_hbm, member_ref), (order_hbm, order_ref),
                (emb_hbm, emb_ref),
            ]
        )
    ]
    for load in loads:
        load.start()
    rows = emb_ref.shape[0]
    features = emb_ref.shape[1]
    slots = n * cap
    per_tile = 128 // cap
    tiles = slots // 128

    barrier = pltpu.get_barrier_semaphore()
    for k in range(1, n):
        pl.semaphore_signal(
            barrier, inc=1, device_id={"shard": peers[k]}, device_id_type=MESH
        )

    for load in loads[:3]:
        load.wait()
    dest = dest_ref[...]
    owner_table = (lax.broadcasted_iota(jnp.int32, (n, rows), 0) == dest).astype(F32)
    before = (
        lax.broadcasted_iota(jnp.int32, (rows, rows), 0)
        < lax.broadcasted_iota(jnp.int32, (rows, rows), 1)
    ).astype(F32).astype(BF16)
    earlier = jnp.dot(owner_table.astype(BF16), before, preferred_element_type=F32)
    rank = jnp.sum(earlier * owner_table, axis=0, keepdims=True).astype(jnp.int32)
    slot = jnp.bitwise_xor(dest, me) * cap + rank
    pack[...] = (
        lax.broadcasted_iota(jnp.int32, (slots, rows), 0) == slot
    ).astype(F32).astype(BF16)

    part = lax.broadcasted_iota(jnp.int32, (8, rows), 0)
    order = order_ref[...]
    fields = jnp.where(
        part == 0,
        member_ref[...] + 1,
        jnp.where(part == 1, order // 128, jnp.where(part == 2, order % 128, 0)),
    ).astype(F32).astype(BF16)
    packed = lax.dot_general(
        fields, pack[...], (((1,), (1,)), ((), ())), preferred_element_type=F32
    )
    key_row = packed[0:1] * float(ORDER_SPAN) + packed[1:2] * 128.0 + packed[2:3]
    for t in range(tiles):
        keys_out[t] = jnp.broadcast_to(key_row[:, t * 128:(t + 1) * 128], (8, 128))

    loads[3].wait()
    x = emb_ref[...]
    squares = jnp.sum(x * x, axis=1, keepdims=True)
    unit[...] = (x * lax.rsqrt(squares + EPSILON)).astype(BF16)

    pl.semaphore_wait(barrier, n - 1)

    def copy(src, dst, sems, k):
        return pltpu.make_async_remote_copy(
            src_ref=src, dst_ref=dst, send_sem=sems[0].at[k], recv_sem=sems[1].at[k],
            device_id={"shard": peers[k]}, device_id_type=MESH,
        )

    row_copies, key_copies, best_copies = {}, {}, {}
    for step, t in enumerate(range(tiles)):
        block = jnp.dot(
            pack[t * 128:(t + 1) * 128, :], unit[...], preferred_element_type=F32
        ).astype(BF16)
        send[t * 128:(t + 1) * 128, :] = block
        for k in range(t * per_tile, (t + 1) * per_tile):
            if k == 0:
                recv[0:cap, :] = block[0:cap, :]
                continue
            row_copies[k] = copy(
                send.at[pl.ds(k * cap, cap)], recv.at[pl.ds(k * cap, cap)],
                (row_send, row_recv), k,
            )
            row_copies[k].start()
        if step == 0:
            for k in range(1, n):
                key_copies[k] = copy(
                    keys_out.at[k // per_tile], keys_in.at[k], (key_send, key_recv), k
                )
                key_copies[k].start()

    lane = lax.broadcasted_iota(jnp.int32, (8, 128), 1) // cap

    def gathered(own, arrived):
        result = []
        for t in range(tiles):
            tile = own[t] if t == 0 else arrived[t * per_tile]
            for j in range(1, per_tile):
                tile = jnp.where(lane == j, arrived[t * per_tile + j], tile)
            result.append(tile)
        return result

    for k in range(1, n):
        key_copies[k].wait_recv()
    key_tiles = gathered(keys_out, keys_in)
    key_lanes = jnp.concatenate([tile[0:1] for tile in key_tiles], axis=1)
    cluster_lanes = jnp.floor(key_lanes * (1.0 / ORDER_SPAN))
    base_lanes = cluster_lanes * float(ORDER_SPAN)
    key_cols = [
        jnp.transpose(jnp.broadcast_to(tile[0:1], (128, 128)))[:, 0:1] for tile in key_tiles
    ]

    def tile_max(scores, column, lanes):
        keys, bases = key_lanes[:, lanes], base_lanes[:, lanes]
        column = jnp.broadcast_to(column, scores.shape)
        allowed = (column < keys) & (column >= bases)
        return jnp.max(jnp.where(allowed, scores, -1.0), axis=0, keepdims=True)

    def inner(a, b):
        return lax.dot_general(
            a, b, (((1,), (1,)), ((), ())), preferred_element_type=F32
        )

    best = None
    for t in range(tiles):
        for k in range(max(1, t * per_tile), (t + 1) * per_tile):
            row_copies[k].wait_recv()
        head, here = t * 128, slice(t * 128, (t + 1) * 128)
        ours = tile_max(
            inner(recv[0:head + 128, :], recv[here, :]),
            jnp.concatenate(key_cols[:t + 1], axis=0), here,
        )
        if t == 0:
            best = ours
        else:
            theirs = tile_max(
                inner(recv[here, :], recv[0:head, :]), key_cols[t], slice(0, head)
            )
            best = jnp.concatenate([jnp.maximum(best, theirs), ours], axis=1)
    for t in range(tiles):
        best_out[t] = jnp.broadcast_to(best[:, t * 128:(t + 1) * 128], (8, 128))
    for k in range(1, n):
        best_copies[k] = copy(
            best_out.at[k // per_tile], best_in.at[k], (best_send, best_recv), k
        )
        best_copies[k].start()

    clusters = cent_ref.shape[0]
    wanted = lax.broadcasted_iota(jnp.int32, (clusters, slots), 0).astype(F32) + 1.0
    member_table = (wanted == cluster_lanes).astype(F32).astype(BF16)
    sums = jnp.dot(member_table, recv[...], preferred_element_type=F32)
    cent_ref[...] = sums * lax.rsqrt(
        jnp.sum(sums * sums, axis=1, keepdims=True) * (1.0 / features) + EPSILON
    )

    for k in range(1, n):
        best_copies[k].wait_recv()
    returned = jnp.concatenate(gathered(best_out, best_in), axis=1)
    result = jnp.zeros((8, rows), F32)
    pieces = []
    for _ in range(3):
        piece = returned.astype(BF16)
        pieces.append(piece)
        returned = returned - piece.astype(F32)
    for piece in pieces:
        result = result + jnp.dot(piece, pack[...], preferred_element_type=F32)
    best_ref[...] = result[0:1]

    for k in range(1, n):
        key_copies[k].wait_send()
        row_copies[k].wait_send()
        best_copies[k].wait_send()


def fused(embeddings, dest_owner, member_cluster, order, n, cap):
    rows, features = embeddings.shape
    slots = n * cap
    vmem = pl.BlockSpec(memory_space=pltpu.VMEM)
    best, centroids = pl.pallas_call(
        functools.partial(exchange_kernel, n, cap),
        out_shape=(
            jax.ShapeDtypeStruct((1, rows), F32),
            jax.ShapeDtypeStruct((CL_DEV, features), F32),
        ),
        in_specs=[pl.BlockSpec(memory_space=pltpu.HBM)] * 4,
        out_specs=(vmem, vmem),
        scratch_shapes=[
            pltpu.VMEM((rows, features), BF16),
            pltpu.VMEM((slots, rows), BF16),
            pltpu.VMEM((slots, features), BF16),
            pltpu.VMEM((slots, features), BF16),
            pltpu.VMEM((slots // 128, 8, 128), F32),
            pltpu.VMEM((n, 8, 128), F32),
            pltpu.VMEM((slots // 128, 8, 128), F32),
            pltpu.VMEM((n, 8, 128), F32),
        ] + [pltpu.SemaphoreType.DMA((n,))] * 6 + [
            pltpu.VMEM((rows, features), F32),
            pltpu.VMEM((1, rows), jnp.int32),
            pltpu.VMEM((1, rows), jnp.int32),
            pltpu.VMEM((1, rows), jnp.int32),
            pltpu.SemaphoreType.DMA((4,)),
        ],
        compiler_params=pltpu.CompilerParams(
            collective_id=0, has_side_effects=True, vmem_limit_bytes=32 * 1024 * 1024
        ),
        cost_estimate=pl.CostEstimate(
            flops=2 * slots * features * (rows + slots + CL_DEV),
            bytes_accessed=4 * rows * features,
            transcendentals=rows,
        ),
    )(
        embeddings,
        dest_owner.reshape(1, rows),
        member_cluster.reshape(1, rows),
        order.reshape(1, rows),
    )
    return best.reshape(rows), centroids


def plain(embeddings, dest_owner, member_cluster, order, owners, capacity):
    rows_here, features = embeddings.shape
    slots = owners * capacity
    squares = jnp.sum(embeddings * embeddings, axis=1, keepdims=True)
    unit_rows = (embeddings * lax.rsqrt(squares + EPSILON)).astype(BF16)
    owner_table = (dest_owner[:, None] == jnp.arange(owners, dtype=jnp.int32)[None, :]).astype(F32)
    positions = jnp.arange(rows_here, dtype=jnp.int32)
    before = (positions[:, None] > positions[None, :]).astype(F32)
    earlier = jnp.dot(before, owner_table, precision=lax.Precision.HIGHEST)
    rank = jnp.sum(earlier * owner_table, axis=1).astype(jnp.int32)
    slot_index = dest_owner * capacity + rank
    send_rows = jnp.zeros((slots, features), BF16).at[slot_index].set(unit_rows)
    code = (member_cluster + 1) * ORDER_SPAN + order
    send_code = jnp.zeros((slots,), jnp.int32).at[slot_index].set(code)
    recv_rows = lax.all_to_all(send_rows, "shard", split_axis=0, concat_axis=0, tiled=True)
    recv_code = lax.all_to_all(send_code, "shard", split_axis=0, concat_axis=0, tiled=True)
    recv_cluster = recv_code // ORDER_SPAN
    scores = lax.dot_general(
        recv_rows, recv_rows, (((1,), (1,)), ((), ())), preferred_element_type=F32
    )
    allowed = (recv_cluster[:, None] == recv_cluster[None, :]) & (
        recv_code[None, :] < recv_code[:, None]
    )
    maxima = jnp.max(jnp.where(allowed, scores, F32(-1.0)), axis=1)
    returned = lax.all_to_all(maxima, "shard", split_axis=0, concat_axis=0, tiled=True)
    max_similarity = returned[slot_index]
    wanted = jnp.arange(CL_DEV, dtype=jnp.int32) + 1
    member_table = (wanted[:, None] == recv_cluster[None, :]).astype(BF16)
    sums = jnp.dot(member_table, recv_rows, preferred_element_type=F32)
    centroids = sums * lax.rsqrt(jnp.mean(sums * sums, axis=1, keepdims=True) + EPSILON)
    return (max_similarity, centroids)


def per_device(embeddings, dest_owner, member_cluster, order):
    owners = lax.axis_size("shard")
    capacity = 2 * embeddings.shape[0] // owners
    blocks_tile = capacity % 16 == 0 and 128 % capacity == 0 and owners & (owners - 1) == 0
    body = fused if blocks_tile else plain
    return body(embeddings, dest_owner, member_cluster, order, owners, capacity)


def solution(mesh):
    in_specs = (
        P(("groups", "shard"), None),
        P(("groups", "shard")),
        P(("groups", "shard")),
        P(("groups", "shard")),
    )
    out_specs = (P(("groups", "shard")), P(("groups", "shard"), None))
    return jax.shard_map(
        per_device, mesh=mesh, in_specs=in_specs, out_specs=out_specs, check_vma=False
    )
```

```python
import functools

import jax
import jax.numpy as jnp
from jax import lax
from jax.experimental import pallas as pl
from jax.experimental.pallas import tpu as pltpu
from jax.sharding import PartitionSpec as P

CL_DEV = 32
EPSILON = 1e-06
ORDER_SPAN = 32768
OVER = 48
MESH = pl.DeviceIdType.MESH
F32 = jnp.float32
BF16 = jnp.bfloat16


def flipped(me, n):
    steps = []
    bit = 1
    while bit < n:
        steps.append(bit * (1 - 2 * lax.rem(lax.div(me, bit), 2)))
        bit *= 2
    peers = [me]
    for step in steps:
        peers = peers + [peer + step for peer in peers]
    return peers


def relay_kernel(
    n, cap,
    emb_hbm, dest_hbm, member_hbm, order_hbm,
    best_ref, cent_ref, flag_ref,
    unit, pack, send, recv, keys_out, keys_in, best_out, best_in,
    row_send, row_recv, key_send, key_recv, best_send, best_recv,
    emb_ref, dest_ref, member_ref, order_ref, load_sem,
    over_out, over_in, place_out, place_in, relay, flag_out, flag_in,
    over_sem, place_sem, relay_send, relay_recv, flag_sem,
):
    me = lax.axis_index("shard")
    peers = flipped(me, n)
    loads = [
        pltpu.make_async_copy(src, dst, load_sem.at[i])
        for i, (src, dst) in enumerate(
            [
                (dest_hbm, dest_ref), (member_hbm, member_ref), (order_hbm, order_ref),
                (emb_hbm, emb_ref),
            ]
        )
    ]
    for load in loads:
        load.start()
    rows = emb_ref.shape[0]
    features = emb_ref.shape[1]
    slots = n * cap
    per_tile = 128 // cap
    half, part_cap = n // 2, cap // 2
    tiles = slots // 128

    barrier = pltpu.get_barrier_semaphore()
    for k in range(1, n):
        pl.semaphore_signal(
            barrier, inc=1, device_id={"shard": peers[k]}, device_id_type=MESH
        )

    across = {"groups": 1 - lax.axis_index("groups")}
    pl.semaphore_signal(barrier, inc=1, device_id=across, device_id_type=MESH)

    for load in loads[:3]:
        load.wait()
    dest = dest_ref[...]
    owner_table = (lax.broadcasted_iota(jnp.int32, (n, rows), 0) == dest).astype(F32)
    before = (
        lax.broadcasted_iota(jnp.int32, (rows, rows), 0)
        < lax.broadcasted_iota(jnp.int32, (rows, rows), 1)
    ).astype(F32).astype(BF16)
    earlier = jnp.dot(owner_table.astype(BF16), before, preferred_element_type=F32)
    rank = jnp.sum(earlier * owner_table, axis=0, keepdims=True).astype(jnp.int32)
    hop = jnp.bitwise_xor(dest, me)
    over = (hop >= half) & (rank >= part_cap)
    slot = jnp.where(
        hop < half,
        hop * cap + rank,
        half * cap + (hop - half) * part_cap + rank
        + jnp.where(over, half * part_cap - part_cap, 0),
    )
    over_row = over.astype(F32)
    over_rank = jnp.dot(
        jnp.broadcast_to(over_row, (8, rows)).astype(BF16), before,
        preferred_element_type=F32,
    )[0:1]
    over_count = jnp.sum(over_row, axis=1, keepdims=True)
    flag = (over_count > float(OVER)).astype(F32)
    pick = (
        (lax.broadcasted_iota(jnp.int32, (128, rows), 0).astype(F32) == over_rank)
        & (over_row > 0.5)
    ).astype(F32).astype(BF16)
    place = (hop - half) * part_cap + rank - part_cap + 1
    place = lax.dot_general(
        jnp.broadcast_to(place, (8, rows)).astype(F32).astype(BF16), pick,
        (((1,), (1,)), ((), ())), preferred_element_type=F32,
    )
    place_out[...] = place - 1.0
    pack[...] = (
        lax.broadcasted_iota(jnp.int32, (slots, rows), 0) == slot
    ).astype(F32).astype(BF16)

    part = lax.broadcasted_iota(jnp.int32, (8, rows), 0)
    order = order_ref[...]
    fields = jnp.where(
        part == 0,
        member_ref[...] + 1,
        jnp.where(part == 1, order // 128, jnp.where(part == 2, order % 128, 0)),
    ).astype(F32).astype(BF16)
    packed = lax.dot_general(
        fields, pack[...], (((1,), (1,)), ((), ())), preferred_element_type=F32
    )
    key_row = packed[0:1] * float(ORDER_SPAN) + packed[1:2] * 128.0 + packed[2:3]
    for t in range(tiles):
        keys_out[t] = jnp.where(
            lax.broadcasted_iota(jnp.int32, (8, 128), 0) == 0,
            jnp.broadcast_to(key_row[:, t * 128:(t + 1) * 128], (8, 128)),
            jnp.broadcast_to(flag, (8, 128)),
        )

    loads[3].wait()
    x = emb_ref[...]
    squares = jnp.sum(x * x, axis=1, keepdims=True)
    unit[...] = (x * lax.rsqrt(squares + EPSILON)).astype(BF16)

    pl.semaphore_wait(barrier, n)

    def copy(src, dst, sends, recvs, k):
        return pltpu.make_async_remote_copy(
            src_ref=src, dst_ref=dst, send_sem=sends, recv_sem=recvs,
            device_id={"shard": peers[k]}, device_id_type=MESH,
        )

    def tiles_of(k):
        return (k // per_tile, 1) if k < half else (2, 2)

    def rows_of(k):
        if k < half:
            return pl.ds(k * cap, cap)
        return pl.ds(half * cap + (k - half) * part_cap, part_cap)

    over_out[...] = jnp.dot(
        pick[0:OVER, :], unit[...], preferred_element_type=F32
    ).astype(BF16)
    over_copy = copy(over_out, over_in, over_sem.at[0], over_sem.at[1], half)
    place_copy = copy(place_out, place_in, place_sem.at[0], place_sem.at[1], half)
    place_copy.start()
    over_copy.start()
    row_copies, key_copies, best_copies, relays = {}, {}, {}, {}
    for step, t in enumerate((2, 0, 1)):
        block = jnp.dot(
            pack[t * 128:(t + 1) * 128, :], unit[...], preferred_element_type=F32
        ).astype(BF16)
        send[t * 128:(t + 1) * 128, :] = block
        if t == 0:
            recv[0:cap, :] = block[0:cap, :]
        for k in range(1, n):
            if tiles_of(k)[0] != t:
                continue
            row_copies[k] = copy(
                send.at[rows_of(k)], recv.at[rows_of(k)],
                row_send.at[k], row_recv.at[k], k,
            )
            row_copies[k].start()
        if step == 0:
            for k in range(1, n):
                first, count = tiles_of(k)
                key_copies[k] = copy(
                    keys_out.at[pl.ds(first, count)], keys_in.at[k, pl.ds(0, count)],
                    key_send.at[k], key_recv.at[k], k,
                )
                key_copies[k].start()

    place_copy.wait_recv()
    over_copy.wait_recv()
    spread = (
        lax.broadcasted_iota(jnp.int32, (128, OVER), 0).astype(F32)
        == place_in[0:1, 0:OVER]
    ).astype(F32).astype(BF16)
    block = jnp.dot(spread, over_in[...], preferred_element_type=F32).astype(BF16)
    relay[...] = block
    extra = 3 * 128
    recv[extra:extra + part_cap, :] = block[0:part_cap, :]
    for k in range(1, half):
        relays[k] = copy(
            relay.at[pl.ds(k * part_cap, part_cap)],
            recv.at[pl.ds(extra + k * part_cap, part_cap)],
            relay_send.at[k], relay_recv.at[k], k,
        )
        relays[k].start()

    lane = lax.broadcasted_iota(jnp.int32, (8, 128), 1)

    def gathered(own, arrived):
        result = []
        for t in range(2):
            tile = own[t] if t == 0 else arrived[t * per_tile, 0]
            for j in range(1, per_tile):
                tile = jnp.where(lane // cap == j, arrived[t * per_tile + j, 0], tile)
            result.append(tile)
        for t in range(2):
            tile = arrived[half, t]
            for j in range(1, half):
                tile = jnp.where(lane // part_cap == j, arrived[half + j, t], tile)
            result.append(tile)
        return result

    for k in range(1, n):
        key_copies[k].wait_recv()
    key_tiles = gathered(keys_out, keys_in)
    seen = keys_out[0]
    for k in range(1, n):
        seen = jnp.maximum(seen, keys_in[k, 0])
    flag_out[...] = jnp.broadcast_to(seen[1:2], (8, 128))
    flag_copy = pltpu.make_async_remote_copy(
        src_ref=flag_out, dst_ref=flag_in, send_sem=flag_sem.at[0],
        recv_sem=flag_sem.at[1], device_id=across, device_id_type=MESH,
    )
    flag_copy.start()
    key_lanes = jnp.concatenate([tile[0:1] for tile in key_tiles], axis=1)
    cluster_lanes = jnp.floor(key_lanes * (1.0 / ORDER_SPAN))
    base_lanes = cluster_lanes * float(ORDER_SPAN)
    key_cols = [
        jnp.transpose(jnp.broadcast_to(tile[0:1], (128, 128)))[:, 0:1] for tile in key_tiles
    ]

    def tile_max(scores, column, lanes):
        keys, bases = key_lanes[:, lanes], base_lanes[:, lanes]
        column = jnp.broadcast_to(column, scores.shape)
        allowed = (column < keys) & (column >= bases)
        return jnp.max(jnp.where(allowed, scores, -1.0), axis=0, keepdims=True)

    def inner(a, b):
        return lax.dot_general(
            a, b, (((1,), (1,)), ((), ())), preferred_element_type=F32
        )

    best = None
    for t in range(tiles):
        if t == 3:
            for k in range(1, half):
                relays[k].wait_recv()
        for k in range(1, n):
            if tiles_of(k)[0] == t:
                row_copies[k].wait_recv()
        head, here = t * 128, slice(t * 128, (t + 1) * 128)
        ours = tile_max(
            inner(recv[0:head + 128, :], recv[here, :]),
            jnp.concatenate(key_cols[:t + 1], axis=0), here,
        )
        if t == 0:
            best = ours
        else:
            theirs = tile_max(
                inner(recv[here, :], recv[0:head, :]), key_cols[t], slice(0, head)
            )
            best = jnp.concatenate([jnp.maximum(best, theirs), ours], axis=1)
    for t in range(tiles):
        best_out[t] = jnp.broadcast_to(best[:, t * 128:(t + 1) * 128], (8, 128))
    for k in range(1, n):
        first, count = tiles_of(k)
        best_copies[k] = copy(
            best_out.at[pl.ds(first, count)], best_in.at[k, pl.ds(0, count)],
            best_send.at[k], best_recv.at[k], k,
        )
        best_copies[k].start()

    clusters = cent_ref.shape[0]
    wanted = lax.broadcasted_iota(jnp.int32, (clusters, slots), 0).astype(F32) + 1.0
    member_table = (wanted == cluster_lanes).astype(F32).astype(BF16)
    sums = jnp.dot(member_table, recv[...], preferred_element_type=F32)
    cent_ref[...] = sums * lax.rsqrt(
        jnp.sum(sums * sums, axis=1, keepdims=True) * (1.0 / features) + EPSILON
    )

    for k in range(1, n):
        best_copies[k].wait_recv()
    returned = jnp.concatenate(gathered(best_out, best_in), axis=1)
    result = jnp.zeros((8, rows), F32)
    pieces = []
    for _ in range(3):
        piece = returned.astype(BF16)
        pieces.append(piece)
        returned = returned - piece.astype(F32)
    for piece in pieces:
        result = result + jnp.dot(piece, pack[...], preferred_element_type=F32)
    best_ref[...] = result[0:1]
    flag_copy.wait()
    flag_ref[...] = jnp.maximum(flag_out[...], flag_in[...])
    over_copy.wait_send()
    place_copy.wait_send()
    for k in range(1, half):
        relays[k].wait_send()

    for k in range(1, n):
        key_copies[k].wait_send()
        row_copies[k].wait_send()
        best_copies[k].wait_send()


def exchange_kernel(
    n, cap,
    emb_hbm, dest_hbm, member_hbm, order_hbm,
    best_ref, cent_ref,
    unit, pack, send, recv, keys_out, keys_in, best_out, best_in,
    row_send, row_recv, key_send, key_recv, best_send, best_recv,
    emb_ref, dest_ref, member_ref, order_ref, load_sem,
):
    me = lax.axis_index("shard")
    peers = flipped(me, n)
    loads = [
        pltpu.make_async_copy(src, dst, load_sem.at[i])
        for i, (src, dst) in enumerate(
            [
                (dest_hbm, dest_ref), (member_hbm, member_ref), (order_hbm, order_ref),
                (emb_hbm, emb_ref),
            ]
        )
    ]
    for load in loads:
        load.start()
    rows = emb_ref.shape[0]
    features = emb_ref.shape[1]
    slots = n * cap
    per_tile = 128 // cap
    tiles = slots // 128

    barrier = pltpu.get_barrier_semaphore()
    for k in range(1, n):
        pl.semaphore_signal(
            barrier, inc=1, device_id={"shard": peers[k]}, device_id_type=MESH
        )

    for load in loads[:3]:
        load.wait()
    dest = dest_ref[...]
    owner_table = (lax.broadcasted_iota(jnp.int32, (n, rows), 0) == dest).astype(F32)
    before = (
        lax.broadcasted_iota(jnp.int32, (rows, rows), 0)
        < lax.broadcasted_iota(jnp.int32, (rows, rows), 1)
    ).astype(F32).astype(BF16)
    earlier = jnp.dot(owner_table.astype(BF16), before, preferred_element_type=F32)
    rank = jnp.sum(earlier * owner_table, axis=0, keepdims=True).astype(jnp.int32)
    slot = jnp.bitwise_xor(dest, me) * cap + rank
    pack[...] = (
        lax.broadcasted_iota(jnp.int32, (slots, rows), 0) == slot
    ).astype(F32).astype(BF16)

    part = lax.broadcasted_iota(jnp.int32, (8, rows), 0)
    order = order_ref[...]
    fields = jnp.where(
        part == 0,
        member_ref[...] + 1,
        jnp.where(part == 1, order // 128, jnp.where(part == 2, order % 128, 0)),
    ).astype(F32).astype(BF16)
    packed = lax.dot_general(
        fields, pack[...], (((1,), (1,)), ((), ())), preferred_element_type=F32
    )
    key_row = packed[0:1] * float(ORDER_SPAN) + packed[1:2] * 128.0 + packed[2:3]
    for t in range(tiles):
        keys_out[t] = jnp.broadcast_to(key_row[:, t * 128:(t + 1) * 128], (8, 128))

    loads[3].wait()
    x = emb_ref[...]
    squares = jnp.sum(x * x, axis=1, keepdims=True)
    unit[...] = (x * lax.rsqrt(squares + EPSILON)).astype(BF16)

    pl.semaphore_wait(barrier, n - 1)

    def copy(src, dst, sems, k):
        return pltpu.make_async_remote_copy(
            src_ref=src, dst_ref=dst, send_sem=sems[0].at[k], recv_sem=sems[1].at[k],
            device_id={"shard": peers[k]}, device_id_type=MESH,
        )

    row_copies, key_copies, best_copies = {}, {}, {}
    for step, t in enumerate(range(tiles)):
        block = jnp.dot(
            pack[t * 128:(t + 1) * 128, :], unit[...], preferred_element_type=F32
        ).astype(BF16)
        send[t * 128:(t + 1) * 128, :] = block
        for k in range(t * per_tile, (t + 1) * per_tile):
            if k == 0:
                recv[0:cap, :] = block[0:cap, :]
                continue
            row_copies[k] = copy(
                send.at[pl.ds(k * cap, cap)], recv.at[pl.ds(k * cap, cap)],
                (row_send, row_recv), k,
            )
            row_copies[k].start()
        if step == 0:
            for k in range(1, n):
                key_copies[k] = copy(
                    keys_out.at[k // per_tile], keys_in.at[k], (key_send, key_recv), k
                )
                key_copies[k].start()

    lane = lax.broadcasted_iota(jnp.int32, (8, 128), 1) // cap

    def gathered(own, arrived):
        result = []
        for t in range(tiles):
            tile = own[t] if t == 0 else arrived[t * per_tile]
            for j in range(1, per_tile):
                tile = jnp.where(lane == j, arrived[t * per_tile + j], tile)
            result.append(tile)
        return result

    for k in range(1, n):
        key_copies[k].wait_recv()
    key_tiles = gathered(keys_out, keys_in)
    key_lanes = jnp.concatenate([tile[0:1] for tile in key_tiles], axis=1)
    cluster_lanes = jnp.floor(key_lanes * (1.0 / ORDER_SPAN))
    base_lanes = cluster_lanes * float(ORDER_SPAN)
    key_cols = [
        jnp.transpose(jnp.broadcast_to(tile[0:1], (128, 128)))[:, 0:1] for tile in key_tiles
    ]

    def tile_max(scores, column, lanes):
        keys, bases = key_lanes[:, lanes], base_lanes[:, lanes]
        column = jnp.broadcast_to(column, scores.shape)
        allowed = (column < keys) & (column >= bases)
        return jnp.max(jnp.where(allowed, scores, -1.0), axis=0, keepdims=True)

    def inner(a, b):
        return lax.dot_general(
            a, b, (((1,), (1,)), ((), ())), preferred_element_type=F32
        )

    best = None
    for t in range(tiles):
        for k in range(max(1, t * per_tile), (t + 1) * per_tile):
            row_copies[k].wait_recv()
        head, here = t * 128, slice(t * 128, (t + 1) * 128)
        ours = tile_max(
            inner(recv[0:head + 128, :], recv[here, :]),
            jnp.concatenate(key_cols[:t + 1], axis=0), here,
        )
        if t == 0:
            best = ours
        else:
            theirs = tile_max(
                inner(recv[here, :], recv[0:head, :]), key_cols[t], slice(0, head)
            )
            best = jnp.concatenate([jnp.maximum(best, theirs), ours], axis=1)
    for t in range(tiles):
        best_out[t] = jnp.broadcast_to(best[:, t * 128:(t + 1) * 128], (8, 128))
    for k in range(1, n):
        best_copies[k] = copy(
            best_out.at[k // per_tile], best_in.at[k], (best_send, best_recv), k
        )
        best_copies[k].start()

    clusters = cent_ref.shape[0]
    wanted = lax.broadcasted_iota(jnp.int32, (clusters, slots), 0).astype(F32) + 1.0
    member_table = (wanted == cluster_lanes).astype(F32).astype(BF16)
    sums = jnp.dot(member_table, recv[...], preferred_element_type=F32)
    cent_ref[...] = sums * lax.rsqrt(
        jnp.sum(sums * sums, axis=1, keepdims=True) * (1.0 / features) + EPSILON
    )

    for k in range(1, n):
        best_copies[k].wait_recv()
    returned = jnp.concatenate(gathered(best_out, best_in), axis=1)
    result = jnp.zeros((8, rows), F32)
    pieces = []
    for _ in range(3):
        piece = returned.astype(BF16)
        pieces.append(piece)
        returned = returned - piece.astype(F32)
    for piece in pieces:
        result = result + jnp.dot(piece, pack[...], preferred_element_type=F32)
    best_ref[...] = result[0:1]

    for k in range(1, n):
        key_copies[k].wait_send()
        row_copies[k].wait_send()
        best_copies[k].wait_send()


def fused(embeddings, dest_owner, member_cluster, order, n, cap):
    rows, features = embeddings.shape
    slots = n * cap
    vmem = pl.BlockSpec(memory_space=pltpu.VMEM)
    best, centroids = pl.pallas_call(
        functools.partial(exchange_kernel, n, cap),
        out_shape=(
            jax.ShapeDtypeStruct((1, rows), F32),
            jax.ShapeDtypeStruct((CL_DEV, features), F32),
        ),
        in_specs=[pl.BlockSpec(memory_space=pltpu.HBM)] * 4,
        out_specs=(vmem, vmem),
        scratch_shapes=[
            pltpu.VMEM((rows, features), BF16),
            pltpu.VMEM((slots, rows), BF16),
            pltpu.VMEM((slots, features), BF16),
            pltpu.VMEM((slots, features), BF16),
            pltpu.VMEM((slots // 128, 8, 128), F32),
            pltpu.VMEM((n, 8, 128), F32),
            pltpu.VMEM((slots // 128, 8, 128), F32),
            pltpu.VMEM((n, 8, 128), F32),
        ] + [pltpu.SemaphoreType.DMA((n,))] * 6 + [
            pltpu.VMEM((rows, features), F32),
            pltpu.VMEM((1, rows), jnp.int32),
            pltpu.VMEM((1, rows), jnp.int32),
            pltpu.VMEM((1, rows), jnp.int32),
            pltpu.SemaphoreType.DMA((4,)),
        ],
        compiler_params=pltpu.CompilerParams(
            collective_id=0, has_side_effects=True, vmem_limit_bytes=32 * 1024 * 1024
        ),
        cost_estimate=pl.CostEstimate(
            flops=2 * slots * features * (rows + slots + CL_DEV),
            bytes_accessed=4 * rows * features,
            transcendentals=rows,
        ),
    )(
        embeddings,
        dest_owner.reshape(1, rows),
        member_cluster.reshape(1, rows),
        order.reshape(1, rows),
    )
    return best.reshape(rows), centroids


def relayed(embeddings, dest_owner, member_cluster, order, n, cap):
    rows, features = embeddings.shape
    slots = n * cap
    vmem = pl.BlockSpec(memory_space=pltpu.VMEM)
    best, centroids, flag = pl.pallas_call(
        functools.partial(relay_kernel, n, cap),
        out_shape=(
            jax.ShapeDtypeStruct((1, rows), F32),
            jax.ShapeDtypeStruct((CL_DEV, features), F32),
            jax.ShapeDtypeStruct((8, 128), F32),
        ),
        in_specs=[pl.BlockSpec(memory_space=pltpu.HBM)] * 4,
        out_specs=(vmem, vmem, vmem),
        scratch_shapes=[
            pltpu.VMEM((rows, features), BF16),
            pltpu.VMEM((slots, rows), BF16),
            pltpu.VMEM((slots, features), BF16),
            pltpu.VMEM((slots, features), BF16),
            pltpu.VMEM((slots // 128, 8, 128), F32),
            pltpu.VMEM((n, 2, 8, 128), F32),
            pltpu.VMEM((slots // 128, 8, 128), F32),
            pltpu.VMEM((n, 2, 8, 128), F32),
        ] + [pltpu.SemaphoreType.DMA((n,))] * 6 + [
            pltpu.VMEM((rows, features), F32),
            pltpu.VMEM((1, rows), jnp.int32),
            pltpu.VMEM((1, rows), jnp.int32),
            pltpu.VMEM((1, rows), jnp.int32),
            pltpu.SemaphoreType.DMA((4,)),
            pltpu.VMEM((OVER, features), BF16),
            pltpu.VMEM((OVER, features), BF16),
            pltpu.VMEM((8, 128), F32),
            pltpu.VMEM((8, 128), F32),
            pltpu.VMEM((128, features), BF16),
            pltpu.VMEM((8, 128), F32),
            pltpu.VMEM((8, 128), F32),
            pltpu.SemaphoreType.DMA((2,)),
            pltpu.SemaphoreType.DMA((2,)),
            pltpu.SemaphoreType.DMA((n,)),
            pltpu.SemaphoreType.DMA((n,)),
            pltpu.SemaphoreType.DMA((2,)),
        ],
        compiler_params=pltpu.CompilerParams(
            collective_id=1, has_side_effects=True, vmem_limit_bytes=32 * 1024 * 1024
        ),
        cost_estimate=pl.CostEstimate(
            flops=2 * slots * features * (rows + slots + CL_DEV),
            bytes_accessed=4 * rows * features,
            transcendentals=rows,
        ),
    )(
        embeddings,
        dest_owner.reshape(1, rows),
        member_cluster.reshape(1, rows),
        order.reshape(1, rows),
    )
    return lax.cond(
        flag[0, 0] > 0.5,
        lambda: fused(embeddings, dest_owner, member_cluster, order, n, cap),
        lambda: (best.reshape(rows), centroids),
    )


def plain(embeddings, dest_owner, member_cluster, order, owners, capacity):
    rows_here, features = embeddings.shape
    slots = owners * capacity
    squares = jnp.sum(embeddings * embeddings, axis=1, keepdims=True)
    unit_rows = (embeddings * lax.rsqrt(squares + EPSILON)).astype(BF16)
    owner_table = (dest_owner[:, None] == jnp.arange(owners, dtype=jnp.int32)[None, :]).astype(F32)
    positions = jnp.arange(rows_here, dtype=jnp.int32)
    before = (positions[:, None] > positions[None, :]).astype(F32)
    earlier = jnp.dot(before, owner_table, precision=lax.Precision.HIGHEST)
    rank = jnp.sum(earlier * owner_table, axis=1).astype(jnp.int32)
    slot_index = dest_owner * capacity + rank
    send_rows = jnp.zeros((slots, features), BF16).at[slot_index].set(unit_rows)
    code = (member_cluster + 1) * ORDER_SPAN + order
    send_code = jnp.zeros((slots,), jnp.int32).at[slot_index].set(code)
    recv_rows = lax.all_to_all(send_rows, "shard", split_axis=0, concat_axis=0, tiled=True)
    recv_code = lax.all_to_all(send_code, "shard", split_axis=0, concat_axis=0, tiled=True)
    recv_cluster = recv_code // ORDER_SPAN
    scores = lax.dot_general(
        recv_rows, recv_rows, (((1,), (1,)), ((), ())), preferred_element_type=F32
    )
    allowed = (recv_cluster[:, None] == recv_cluster[None, :]) & (
        recv_code[None, :] < recv_code[:, None]
    )
    maxima = jnp.max(jnp.where(allowed, scores, F32(-1.0)), axis=1)
    returned = lax.all_to_all(maxima, "shard", split_axis=0, concat_axis=0, tiled=True)
    max_similarity = returned[slot_index]
    wanted = jnp.arange(CL_DEV, dtype=jnp.int32) + 1
    member_table = (wanted[:, None] == recv_cluster[None, :]).astype(BF16)
    sums = jnp.dot(member_table, recv_rows, preferred_element_type=F32)
    centroids = sums * lax.rsqrt(jnp.mean(sums * sums, axis=1, keepdims=True) + EPSILON)
    return (max_similarity, centroids)


def per_device(embeddings, dest_owner, member_cluster, order):
    owners = lax.axis_size("shard")
    capacity = 2 * embeddings.shape[0] // owners
    blocks_tile = capacity % 16 == 0 and 128 % capacity == 0 and owners & (owners - 1) == 0
    body = fused if blocks_tile else plain
    if owners == 16 and capacity == 32 and lax.axis_size("groups") == 2:
        body = relayed
    return body(embeddings, dest_owner, member_cluster, order, owners, capacity)


def solution(mesh):
    in_specs = (
        P(("groups", "shard"), None),
        P(("groups", "shard")),
        P(("groups", "shard")),
        P(("groups", "shard")),
    )
    out_specs = (P(("groups", "shard")), P(("groups", "shard"), None))
    return jax.shard_map(
        per_device, mesh=mesh, in_specs=in_specs, out_specs=out_specs, check_vma=False
    )
```

```python
import functools

import jax
import jax.numpy as jnp
from jax import lax
from jax.experimental import pallas as pl
from jax.experimental.pallas import tpu as pltpu
from jax.sharding import PartitionSpec as P

CL_DEV = 32
EPSILON = 1e-06
ORDER_SPAN = 32768
OVER = 48
MESH = pl.DeviceIdType.MESH
F32 = jnp.float32
BF16 = jnp.bfloat16


def flipped(me, n):
    steps = []
    bit = 1
    while bit < n:
        steps.append(bit * (1 - 2 * lax.rem(lax.div(me, bit), 2)))
        bit *= 2
    peers = [me]
    for step in steps:
        peers = peers + [peer + step for peer in peers]
    return peers


def relay_kernel(
    n, cap,
    emb_hbm, dest_hbm, member_hbm, order_hbm,
    best_ref, cent_ref, flag_ref,
    unit, pack, send, recv, keys_out, keys_in, best_out, best_in,
    row_send, row_recv, key_send, key_recv, best_send, best_recv,
    emb_ref, dest_ref, member_ref, order_ref, load_sem,
    over_out, over_in, place_out, place_in, relay, flag_out, flag_in,
    over_sem, place_sem, relay_send, relay_recv, flag_sem,
):
    me = lax.axis_index("shard")
    peers = flipped(me, n)
    loads = [
        pltpu.make_async_copy(src, dst, load_sem.at[i])
        for i, (src, dst) in enumerate(
            [
                (dest_hbm, dest_ref), (member_hbm, member_ref), (order_hbm, order_ref),
                (emb_hbm, emb_ref),
            ]
        )
    ]
    for load in loads:
        load.start()
    rows = emb_ref.shape[0]
    features = emb_ref.shape[1]
    slots = n * cap
    per_tile = 128 // cap
    half, part_cap = n // 2, cap // 2
    tiles = slots // 128

    barrier = pltpu.get_barrier_semaphore()
    for k in range(1, n):
        pl.semaphore_signal(
            barrier, inc=1, device_id={"shard": peers[k]}, device_id_type=MESH
        )

    across = {"groups": 1 - lax.axis_index("groups")}
    pl.semaphore_signal(barrier, inc=1, device_id=across, device_id_type=MESH)

    for load in loads[:3]:
        load.wait()
    dest = dest_ref[...]
    owner_table = (lax.broadcasted_iota(jnp.int32, (n, rows), 0) == dest).astype(F32)
    before = (
        lax.broadcasted_iota(jnp.int32, (rows, rows), 0)
        < lax.broadcasted_iota(jnp.int32, (rows, rows), 1)
    ).astype(F32).astype(BF16)
    earlier = jnp.dot(owner_table.astype(BF16), before, preferred_element_type=F32)
    rank = jnp.sum(earlier * owner_table, axis=0, keepdims=True).astype(jnp.int32)
    hop = jnp.bitwise_xor(dest, me)
    over = (hop >= half) & (rank >= part_cap)
    slot = jnp.where(
        hop < half,
        hop * cap + rank,
        half * cap + (hop - half) * part_cap + rank
        + jnp.where(over, half * part_cap - part_cap, 0),
    )
    over_row = over.astype(F32)
    over_rank = jnp.dot(
        jnp.broadcast_to(over_row, (8, rows)).astype(BF16), before,
        preferred_element_type=F32,
    )[0:1]
    over_count = jnp.sum(over_row, axis=1, keepdims=True)
    flag = (over_count > float(OVER)).astype(F32)
    pick = (
        (lax.broadcasted_iota(jnp.int32, (128, rows), 0).astype(F32) == over_rank)
        & (over_row > 0.5)
    ).astype(F32).astype(BF16)
    place = (hop - half) * part_cap + rank - part_cap + 1
    place = lax.dot_general(
        jnp.broadcast_to(place, (8, rows)).astype(F32).astype(BF16), pick,
        (((1,), (1,)), ((), ())), preferred_element_type=F32,
    )
    place_out[...] = place - 1.0
    pack[...] = (
        lax.broadcasted_iota(jnp.int32, (slots, rows), 0) == slot
    ).astype(F32).astype(BF16)

    part = lax.broadcasted_iota(jnp.int32, (8, rows), 0)
    order = order_ref[...]
    fields = jnp.where(
        part == 0,
        member_ref[...] + 1,
        jnp.where(part == 1, order // 128, jnp.where(part == 2, order % 128, 0)),
    ).astype(F32).astype(BF16)
    packed = lax.dot_general(
        fields, pack[...], (((1,), (1,)), ((), ())), preferred_element_type=F32
    )
    key_row = packed[0:1] * float(ORDER_SPAN) + packed[1:2] * 128.0 + packed[2:3]
    for t in range(tiles):
        keys_out[t] = jnp.where(
            lax.broadcasted_iota(jnp.int32, (8, 128), 0) == 0,
            jnp.broadcast_to(key_row[:, t * 128:(t + 1) * 128], (8, 128)),
            jnp.broadcast_to(flag, (8, 128)),
        )

    loads[3].wait()
    x = emb_ref[...]
    squares = jnp.sum(x * x, axis=1, keepdims=True)
    unit[...] = (x * lax.rsqrt(squares + EPSILON)).astype(BF16)

    pl.semaphore_wait(barrier, n)

    def copy(src, dst, sends, recvs, k):
        return pltpu.make_async_remote_copy(
            src_ref=src, dst_ref=dst, send_sem=sends, recv_sem=recvs,
            device_id={"shard": peers[k]}, device_id_type=MESH,
        )

    def tiles_of(k):
        return (k // per_tile, 1) if k < half else (2, 2)

    def rows_of(k):
        if k < half:
            return pl.ds(k * cap, cap)
        return pl.ds(half * cap + (k - half) * part_cap, part_cap)

    over_out[...] = jnp.dot(
        pick[0:OVER, :], unit[...], preferred_element_type=F32
    ).astype(BF16)
    over_copy = copy(over_out, over_in, over_sem.at[0], over_sem.at[1], half)
    place_copy = copy(place_out, place_in, place_sem.at[0], place_sem.at[1], half)
    place_copy.start()
    over_copy.start()
    row_copies, key_copies, best_copies, relays = {}, {}, {}, {}
    for step, t in enumerate((0, 1, 2)):
        block = jnp.dot(
            pack[t * 128:(t + 1) * 128, :], unit[...], preferred_element_type=F32
        ).astype(BF16)
        send[t * 128:(t + 1) * 128, :] = block
        if t == 0:
            recv[0:cap, :] = block[0:cap, :]
        for k in range(1, n):
            if tiles_of(k)[0] != t:
                continue
            row_copies[k] = copy(
                send.at[rows_of(k)], recv.at[rows_of(k)],
                row_send.at[k], row_recv.at[k], k,
            )
            row_copies[k].start()
        if step == 0:
            for k in range(1, n):
                first, count = tiles_of(k)
                key_copies[k] = copy(
                    keys_out.at[pl.ds(first, count)], keys_in.at[k, pl.ds(0, count)],
                    key_send.at[k], key_recv.at[k], k,
                )
                key_copies[k].start()

    place_copy.wait_recv()
    over_copy.wait_recv()
    spread = (
        lax.broadcasted_iota(jnp.int32, (128, OVER), 0).astype(F32)
        == place_in[0:1, 0:OVER]
    ).astype(F32).astype(BF16)
    block = jnp.dot(spread, over_in[...], preferred_element_type=F32).astype(BF16)
    relay[...] = block
    extra = 3 * 128
    recv[extra:extra + part_cap, :] = block[0:part_cap, :]
    for k in range(1, half):
        relays[k] = copy(
            relay.at[pl.ds(k * part_cap, part_cap)],
            recv.at[pl.ds(extra + k * part_cap, part_cap)],
            relay_send.at[k], relay_recv.at[k], k,
        )
        relays[k].start()

    lane = lax.broadcasted_iota(jnp.int32, (8, 128), 1)

    def gathered(own, arrived):
        result = []
        for t in range(2):
            tile = own[t] if t == 0 else arrived[t * per_tile, 0]
            for j in range(1, per_tile):
                tile = jnp.where(lane // cap == j, arrived[t * per_tile + j, 0], tile)
            result.append(tile)
        for t in range(2):
            tile = arrived[half, t]
            for j in range(1, half):
                tile = jnp.where(lane // part_cap == j, arrived[half + j, t], tile)
            result.append(tile)
        return result

    for k in range(1, n):
        key_copies[k].wait_recv()
    key_tiles = gathered(keys_out, keys_in)
    seen = keys_out[0]
    for k in range(1, n):
        seen = jnp.maximum(seen, keys_in[k, 0])
    flag_out[...] = jnp.broadcast_to(seen[1:2], (8, 128))
    flag_copy = pltpu.make_async_remote_copy(
        src_ref=flag_out, dst_ref=flag_in, send_sem=flag_sem.at[0],
        recv_sem=flag_sem.at[1], device_id=across, device_id_type=MESH,
    )
    flag_copy.start()
    key_lanes = jnp.concatenate([tile[0:1] for tile in key_tiles], axis=1)
    cluster_lanes = jnp.floor(key_lanes * (1.0 / ORDER_SPAN))
    base_lanes = cluster_lanes * float(ORDER_SPAN)
    key_cols = [
        jnp.transpose(jnp.broadcast_to(tile[0:1], (128, 128)))[:, 0:1] for tile in key_tiles
    ]

    def tile_max(scores, column, lanes):
        keys, bases = key_lanes[:, lanes], base_lanes[:, lanes]
        column = jnp.broadcast_to(column, scores.shape)
        allowed = (column < keys) & (column >= bases)
        return jnp.max(jnp.where(allowed, scores, -1.0), axis=0, keepdims=True)

    def inner(a, b):
        return lax.dot_general(
            a, b, (((1,), (1,)), ((), ())), preferred_element_type=F32
        )

    best = None
    for t in range(tiles):
        if t == 3:
            for k in range(1, half):
                relays[k].wait_recv()
        for k in range(1, n):
            if tiles_of(k)[0] == t:
                row_copies[k].wait_recv()
        head, here = t * 128, slice(t * 128, (t + 1) * 128)
        ours = tile_max(
            inner(recv[0:head + 128, :], recv[here, :]),
            jnp.concatenate(key_cols[:t + 1], axis=0), here,
        )
        if t == 0:
            best = ours
        else:
            theirs = tile_max(
                inner(recv[here, :], recv[0:head, :]), key_cols[t], slice(0, head)
            )
            best = jnp.concatenate([jnp.maximum(best, theirs), ours], axis=1)
    for t in range(tiles):
        best_out[t] = jnp.broadcast_to(best[:, t * 128:(t + 1) * 128], (8, 128))
    for k in range(1, n):
        first, count = tiles_of(k)
        best_copies[k] = copy(
            best_out.at[pl.ds(first, count)], best_in.at[k, pl.ds(0, count)],
            best_send.at[k], best_recv.at[k], k,
        )
        best_copies[k].start()

    clusters = cent_ref.shape[0]
    wanted = lax.broadcasted_iota(jnp.int32, (clusters, slots), 0).astype(F32) + 1.0
    member_table = (wanted == cluster_lanes).astype(F32).astype(BF16)
    sums = jnp.dot(member_table, recv[...], preferred_element_type=F32)
    cent_ref[...] = sums * lax.rsqrt(
        jnp.sum(sums * sums, axis=1, keepdims=True) * (1.0 / features) + EPSILON
    )

    flag_copy.wait()
    flag_ref[0] = jnp.max(jnp.maximum(flag_out[...], flag_in[...])).astype(jnp.int32)
    for k in range(1, n):
        best_copies[k].wait_recv()
    returned = jnp.concatenate(gathered(best_out, best_in), axis=1)
    result = jnp.zeros((8, rows), F32)
    pieces = []
    for _ in range(3):
        piece = returned.astype(BF16)
        pieces.append(piece)
        returned = returned - piece.astype(F32)
    for piece in pieces:
        result = result + jnp.dot(piece, pack[...], preferred_element_type=F32)
    best_ref[...] = result[0:1]
    over_copy.wait_send()
    place_copy.wait_send()
    for k in range(1, half):
        relays[k].wait_send()

    for k in range(1, n):
        key_copies[k].wait_send()
        row_copies[k].wait_send()
        best_copies[k].wait_send()


def exchange_kernel(
    n, cap,
    emb_hbm, dest_hbm, member_hbm, order_hbm,
    best_ref, cent_ref,
    unit, pack, send, recv, keys_out, keys_in, best_out, best_in,
    row_send, row_recv, key_send, key_recv, best_send, best_recv,
    emb_ref, dest_ref, member_ref, order_ref, load_sem,
):
    me = lax.axis_index("shard")
    peers = flipped(me, n)
    loads = [
        pltpu.make_async_copy(src, dst, load_sem.at[i])
        for i, (src, dst) in enumerate(
            [
                (dest_hbm, dest_ref), (member_hbm, member_ref), (order_hbm, order_ref),
                (emb_hbm, emb_ref),
            ]
        )
    ]
    for load in loads:
        load.start()
    rows = emb_ref.shape[0]
    features = emb_ref.shape[1]
    slots = n * cap
    per_tile = 128 // cap
    tiles = slots // 128

    barrier = pltpu.get_barrier_semaphore()
    for k in range(1, n):
        pl.semaphore_signal(
            barrier, inc=1, device_id={"shard": peers[k]}, device_id_type=MESH
        )

    for load in loads[:3]:
        load.wait()
    dest = dest_ref[...]
    owner_table = (lax.broadcasted_iota(jnp.int32, (n, rows), 0) == dest).astype(F32)
    before = (
        lax.broadcasted_iota(jnp.int32, (rows, rows), 0)
        < lax.broadcasted_iota(jnp.int32, (rows, rows), 1)
    ).astype(F32).astype(BF16)
    earlier = jnp.dot(owner_table.astype(BF16), before, preferred_element_type=F32)
    rank = jnp.sum(earlier * owner_table, axis=0, keepdims=True).astype(jnp.int32)
    slot = jnp.bitwise_xor(dest, me) * cap + rank
    pack[...] = (
        lax.broadcasted_iota(jnp.int32, (slots, rows), 0) == slot
    ).astype(F32).astype(BF16)

    part = lax.broadcasted_iota(jnp.int32, (8, rows), 0)
    order = order_ref[...]
    fields = jnp.where(
        part == 0,
        member_ref[...] + 1,
        jnp.where(part == 1, order // 128, jnp.where(part == 2, order % 128, 0)),
    ).astype(F32).astype(BF16)
    packed = lax.dot_general(
        fields, pack[...], (((1,), (1,)), ((), ())), preferred_element_type=F32
    )
    key_row = packed[0:1] * float(ORDER_SPAN) + packed[1:2] * 128.0 + packed[2:3]
    for t in range(tiles):
        keys_out[t] = jnp.broadcast_to(key_row[:, t * 128:(t + 1) * 128], (8, 128))

    loads[3].wait()
    x = emb_ref[...]
    squares = jnp.sum(x * x, axis=1, keepdims=True)
    unit[...] = (x * lax.rsqrt(squares + EPSILON)).astype(BF16)

    pl.semaphore_wait(barrier, n - 1)

    def copy(src, dst, sems, k):
        return pltpu.make_async_remote_copy(
            src_ref=src, dst_ref=dst, send_sem=sems[0].at[k], recv_sem=sems[1].at[k],
            device_id={"shard": peers[k]}, device_id_type=MESH,
        )

    row_copies, key_copies, best_copies = {}, {}, {}
    for step, t in enumerate(range(tiles)):
        block = jnp.dot(
            pack[t * 128:(t + 1) * 128, :], unit[...], preferred_element_type=F32
        ).astype(BF16)
        send[t * 128:(t + 1) * 128, :] = block
        for k in range(t * per_tile, (t + 1) * per_tile):
            if k == 0:
                recv[0:cap, :] = block[0:cap, :]
                continue
            row_copies[k] = copy(
                send.at[pl.ds(k * cap, cap)], recv.at[pl.ds(k * cap, cap)],
                (row_send, row_recv), k,
            )
            row_copies[k].start()
        if step == 0:
            for k in range(1, n):
                key_copies[k] = copy(
                    keys_out.at[k // per_tile], keys_in.at[k], (key_send, key_recv), k
                )
                key_copies[k].start()

    lane = lax.broadcasted_iota(jnp.int32, (8, 128), 1) // cap

    def gathered(own, arrived):
        result = []
        for t in range(tiles):
            tile = own[t] if t == 0 else arrived[t * per_tile]
            for j in range(1, per_tile):
                tile = jnp.where(lane == j, arrived[t * per_tile + j], tile)
            result.append(tile)
        return result

    for k in range(1, n):
        key_copies[k].wait_recv()
    key_tiles = gathered(keys_out, keys_in)
    key_lanes = jnp.concatenate([tile[0:1] for tile in key_tiles], axis=1)
    cluster_lanes = jnp.floor(key_lanes * (1.0 / ORDER_SPAN))
    base_lanes = cluster_lanes * float(ORDER_SPAN)
    key_cols = [
        jnp.transpose(jnp.broadcast_to(tile[0:1], (128, 128)))[:, 0:1] for tile in key_tiles
    ]

    def tile_max(scores, column, lanes):
        keys, bases = key_lanes[:, lanes], base_lanes[:, lanes]
        column = jnp.broadcast_to(column, scores.shape)
        allowed = (column < keys) & (column >= bases)
        return jnp.max(jnp.where(allowed, scores, -1.0), axis=0, keepdims=True)

    def inner(a, b):
        return lax.dot_general(
            a, b, (((1,), (1,)), ((), ())), preferred_element_type=F32
        )

    best = None
    for t in range(tiles):
        for k in range(max(1, t * per_tile), (t + 1) * per_tile):
            row_copies[k].wait_recv()
        head, here = t * 128, slice(t * 128, (t + 1) * 128)
        ours = tile_max(
            inner(recv[0:head + 128, :], recv[here, :]),
            jnp.concatenate(key_cols[:t + 1], axis=0), here,
        )
        if t == 0:
            best = ours
        else:
            theirs = tile_max(
                inner(recv[here, :], recv[0:head, :]), key_cols[t], slice(0, head)
            )
            best = jnp.concatenate([jnp.maximum(best, theirs), ours], axis=1)
    for t in range(tiles):
        best_out[t] = jnp.broadcast_to(best[:, t * 128:(t + 1) * 128], (8, 128))
    for k in range(1, n):
        best_copies[k] = copy(
            best_out.at[k // per_tile], best_in.at[k], (best_send, best_recv), k
        )
        best_copies[k].start()

    clusters = cent_ref.shape[0]
    wanted = lax.broadcasted_iota(jnp.int32, (clusters, slots), 0).astype(F32) + 1.0
    member_table = (wanted == cluster_lanes).astype(F32).astype(BF16)
    sums = jnp.dot(member_table, recv[...], preferred_element_type=F32)
    cent_ref[...] = sums * lax.rsqrt(
        jnp.sum(sums * sums, axis=1, keepdims=True) * (1.0 / features) + EPSILON
    )

    for k in range(1, n):
        best_copies[k].wait_recv()
    returned = jnp.concatenate(gathered(best_out, best_in), axis=1)
    result = jnp.zeros((8, rows), F32)
    pieces = []
    for _ in range(3):
        piece = returned.astype(BF16)
        pieces.append(piece)
        returned = returned - piece.astype(F32)
    for piece in pieces:
        result = result + jnp.dot(piece, pack[...], preferred_element_type=F32)
    best_ref[...] = result[0:1]

    for k in range(1, n):
        key_copies[k].wait_send()
        row_copies[k].wait_send()
        best_copies[k].wait_send()


def fused(embeddings, dest_owner, member_cluster, order, n, cap):
    rows, features = embeddings.shape
    slots = n * cap
    vmem = pl.BlockSpec(memory_space=pltpu.VMEM)
    best, centroids = pl.pallas_call(
        functools.partial(exchange_kernel, n, cap),
        out_shape=(
            jax.ShapeDtypeStruct((1, rows), F32),
            jax.ShapeDtypeStruct((CL_DEV, features), F32),
        ),
        in_specs=[pl.BlockSpec(memory_space=pltpu.HBM)] * 4,
        out_specs=(vmem, vmem),
        scratch_shapes=[
            pltpu.VMEM((rows, features), BF16),
            pltpu.VMEM((slots, rows), BF16),
            pltpu.VMEM((slots, features), BF16),
            pltpu.VMEM((slots, features), BF16),
            pltpu.VMEM((slots // 128, 8, 128), F32),
            pltpu.VMEM((n, 8, 128), F32),
            pltpu.VMEM((slots // 128, 8, 128), F32),
            pltpu.VMEM((n, 8, 128), F32),
        ] + [pltpu.SemaphoreType.DMA((n,))] * 6 + [
            pltpu.VMEM((rows, features), F32),
            pltpu.VMEM((1, rows), jnp.int32),
            pltpu.VMEM((1, rows), jnp.int32),
            pltpu.VMEM((1, rows), jnp.int32),
            pltpu.SemaphoreType.DMA((4,)),
        ],
        compiler_params=pltpu.CompilerParams(
            collective_id=0, has_side_effects=True, vmem_limit_bytes=32 * 1024 * 1024
        ),
        cost_estimate=pl.CostEstimate(
            flops=2 * slots * features * (rows + slots + CL_DEV),
            bytes_accessed=4 * rows * features,
            transcendentals=rows,
        ),
    )(
        embeddings,
        dest_owner.reshape(1, rows),
        member_cluster.reshape(1, rows),
        order.reshape(1, rows),
    )
    return best.reshape(rows), centroids


def relayed(embeddings, dest_owner, member_cluster, order, n, cap):
    rows, features = embeddings.shape
    slots = n * cap
    vmem = pl.BlockSpec(memory_space=pltpu.VMEM)
    best, centroids, flag = pl.pallas_call(
        functools.partial(relay_kernel, n, cap),
        out_shape=(
            jax.ShapeDtypeStruct((1, rows), F32),
            jax.ShapeDtypeStruct((CL_DEV, features), F32),
            jax.ShapeDtypeStruct((1,), jnp.int32),
        ),
        in_specs=[pl.BlockSpec(memory_space=pltpu.HBM)] * 4,
        out_specs=(vmem, vmem, pl.BlockSpec(memory_space=pltpu.SMEM)),
        scratch_shapes=[
            pltpu.VMEM((rows, features), BF16),
            pltpu.VMEM((slots, rows), BF16),
            pltpu.VMEM((slots, features), BF16),
            pltpu.VMEM((slots, features), BF16),
            pltpu.VMEM((slots // 128, 8, 128), F32),
            pltpu.VMEM((n, 2, 8, 128), F32),
            pltpu.VMEM((slots // 128, 8, 128), F32),
            pltpu.VMEM((n, 2, 8, 128), F32),
        ] + [pltpu.SemaphoreType.DMA((n,))] * 6 + [
            pltpu.VMEM((rows, features), F32),
            pltpu.VMEM((1, rows), jnp.int32),
            pltpu.VMEM((1, rows), jnp.int32),
            pltpu.VMEM((1, rows), jnp.int32),
            pltpu.SemaphoreType.DMA((4,)),
            pltpu.VMEM((OVER, features), BF16),
            pltpu.VMEM((OVER, features), BF16),
            pltpu.VMEM((8, 128), F32),
            pltpu.VMEM((8, 128), F32),
            pltpu.VMEM((128, features), BF16),
            pltpu.VMEM((8, 128), F32),
            pltpu.VMEM((8, 128), F32),
            pltpu.SemaphoreType.DMA((2,)),
            pltpu.SemaphoreType.DMA((2,)),
            pltpu.SemaphoreType.DMA((n,)),
            pltpu.SemaphoreType.DMA((n,)),
            pltpu.SemaphoreType.DMA((2,)),
        ],
        compiler_params=pltpu.CompilerParams(
            collective_id=1, has_side_effects=True, vmem_limit_bytes=32 * 1024 * 1024
        ),
        cost_estimate=pl.CostEstimate(
            flops=2 * slots * features * (rows + slots + CL_DEV),
            bytes_accessed=4 * rows * features,
            transcendentals=rows,
        ),
    )(
        embeddings,
        dest_owner.reshape(1, rows),
        member_cluster.reshape(1, rows),
        order.reshape(1, rows),
    )
    return lax.cond(
        flag[0] > 0,
        lambda: fused(embeddings, dest_owner, member_cluster, order, n, cap),
        lambda: (best.reshape(rows), centroids),
    )


def plain(embeddings, dest_owner, member_cluster, order, owners, capacity):
    rows_here, features = embeddings.shape
    slots = owners * capacity
    squares = jnp.sum(embeddings * embeddings, axis=1, keepdims=True)
    unit_rows = (embeddings * lax.rsqrt(squares + EPSILON)).astype(BF16)
    owner_table = (dest_owner[:, None] == jnp.arange(owners, dtype=jnp.int32)[None, :]).astype(F32)
    positions = jnp.arange(rows_here, dtype=jnp.int32)
    before = (positions[:, None] > positions[None, :]).astype(F32)
    earlier = jnp.dot(before, owner_table, precision=lax.Precision.HIGHEST)
    rank = jnp.sum(earlier * owner_table, axis=1).astype(jnp.int32)
    slot_index = dest_owner * capacity + rank
    send_rows = jnp.zeros((slots, features), BF16).at[slot_index].set(unit_rows)
    code = (member_cluster + 1) * ORDER_SPAN + order
    send_code = jnp.zeros((slots,), jnp.int32).at[slot_index].set(code)
    recv_rows = lax.all_to_all(send_rows, "shard", split_axis=0, concat_axis=0, tiled=True)
    recv_code = lax.all_to_all(send_code, "shard", split_axis=0, concat_axis=0, tiled=True)
    recv_cluster = recv_code // ORDER_SPAN
    scores = lax.dot_general(
        recv_rows, recv_rows, (((1,), (1,)), ((), ())), preferred_element_type=F32
    )
    allowed = (recv_cluster[:, None] == recv_cluster[None, :]) & (
        recv_code[None, :] < recv_code[:, None]
    )
    maxima = jnp.max(jnp.where(allowed, scores, F32(-1.0)), axis=1)
    returned = lax.all_to_all(maxima, "shard", split_axis=0, concat_axis=0, tiled=True)
    max_similarity = returned[slot_index]
    wanted = jnp.arange(CL_DEV, dtype=jnp.int32) + 1
    member_table = (wanted[:, None] == recv_cluster[None, :]).astype(BF16)
    sums = jnp.dot(member_table, recv_rows, preferred_element_type=F32)
    centroids = sums * lax.rsqrt(jnp.mean(sums * sums, axis=1, keepdims=True) + EPSILON)
    return (max_similarity, centroids)


def per_device(embeddings, dest_owner, member_cluster, order):
    owners = lax.axis_size("shard")
    capacity = 2 * embeddings.shape[0] // owners
    blocks_tile = capacity % 16 == 0 and 128 % capacity == 0 and owners & (owners - 1) == 0
    body = fused if blocks_tile else plain
    if owners == 16 and capacity == 32 and lax.axis_size("groups") == 2:
        body = relayed
    return body(embeddings, dest_owner, member_cluster, order, owners, capacity)


def solution(mesh):
    in_specs = (
        P(("groups", "shard"), None),
        P(("groups", "shard")),
        P(("groups", "shard")),
        P(("groups", "shard")),
    )
    out_specs = (P(("groups", "shard")), P(("groups", "shard"), None))
    return jax.shard_map(
        per_device, mesh=mesh, in_specs=in_specs, out_specs=out_specs, check_vma=False
    )
```
